256 devices in a mesh: row: 16 (over x, y), col: 16 (over z, core).
Axes of the slice: x: 4, y: 4, z: 8, core: 2. Of those that a mesh axis runs over, the one named last changes fastest.
Arguments:
- momentum: float32 [7168, 18432], P('row', 'col'), may hold values from -100 to 100
- gradient: bfloat16 [7168, 18432], P('row', 'col'), may hold values from -6 to 6
- weight: float32 [7168, 18432], P('row', 'col'), may hold values from -6 to 6
- right_factor: float32 [256, 18432], P('row', 'col'), may hold values from -6 to 6
Outputs:
- new_momentum: float32 [7168, 18432], P('row', 'col')
- new_weight: float32 [7168, 18432], P('row', 'col')
- new_factor: float32 [256, 18432], P('row', 'col')
The draws below stay inside these ranges and needn't reach their ends.
All inputs are finite; a program needn't handle non-finite values.
Results may differ from the reference program's by a relative error of at most 0.0003.
Values sent between devices are 32-bit elements; how exact they have to be, the bound alone decides.
No kernel may reach another device: no remote copies, remote signals or barrier semaphores. Data moves between devices by JAX's collectives and lax.ppermute only.
A program may use at most 64 MiB of HBM per device.

```python
import math
import jax
import jax.numpy as jnp
from jax import lax

MDIM = 7168
NDIM = 18432
RANK = 256


def draw_momentum(key, part):
    key = jax.random.fold_in(key, 7)
    streams = jax.random.split(key, 3)
    row_scale = jnp.exp(jax.random.uniform(streams[0], (MDIM, 1), jnp.float32, 0.0, math.log(10.0)))
    col_scale = jnp.exp(jax.random.uniform(streams[1], (1, NDIM), jnp.float32, 0.0, math.log(10.0)))
    row_place = jnp.arange(MDIM, dtype=jnp.float32)[:, None] / (MDIM - 1)
    col_place = jnp.arange(NDIM, dtype=jnp.float32)[None, :] / (NDIM - 1)
    entries = jnp.clip(jax.random.normal(streams[2], (MDIM, NDIM), jnp.float32), -5.0, 5.0)
    growth = math.log(3.0)
    shaped = entries * row_scale * col_scale * jnp.exp(growth * (row_place + col_place)) / 40.0
    return jnp.clip(shaped, -100.0, 100.0)


def steps_of(own_key, extent, cuts, least, high):
    level, own = 1.0, jax.random.fold_in(own_key, 6)
    for position, shards_of in cuts:
        steps = jnp.exp(jax.random.uniform(jax.random.fold_in(own, position), (shards_of,), jnp.float32, least / len(cuts), high / len(cuts)))
        level = level * jnp.repeat(steps, extent[position] // shards_of).reshape([-1 if axis == position else 1 for axis in range(len(extent))])
    return level


def scatter_about(own_key, dims, scale, reach, cuts=(), kind=jnp.bfloat16):
    result = jax.random.normal(own_key, dims, jnp.float32) * scale
    if len(cuts) > 0:
        result = steps_of(own_key, dims, cuts, -0.22, 0.18) * result
    return jnp.clip(result, min=-reach, max=reach).astype(kind)


def setup_inputs(seed: int = 0) -> dict:
    splits = jax.random.split(jax.random.key(seed), 5)
    return {
        "momentum": draw_momentum(jax.random.fold_in(splits[4], 71), 0),
        "gradient": scatter_about(splits[1], (MDIM, NDIM), 1.0, 6.0, ((0, 16), (1, 16))),
        "weight": scatter_about(splits[2], (MDIM, NDIM), 1.0, 6.0, ((0, 16), (1, 16)), jnp.float32),
        "right_factor": scatter_about(splits[3], (RANK, NDIM), 1.0, 6.0, ((0, 16), (1, 16)), jnp.float32),
    }


epsilon = 1e-06
momentum_keep = 0.95
learn_rate = 0.3
weight_decay = 0.1

def reference(momentum, gradient, weight, right_factor):
    highest = lax.Precision.HIGHEST
    summed = momentum + gradient.astype(jnp.float32)
    projected = lax.dot_general(summed.astype(jnp.float32), right_factor.astype(jnp.float32), (((1,), (1,)), ((), ())), precision=highest, preferred_element_type=jnp.float32)
    gram_matrix = lax.dot_general(projected.astype(jnp.float32), projected.astype(jnp.float32), (((0,), (0,)), ((), ())), precision=highest, preferred_element_type=jnp.float32)
    lower_factor = jnp.linalg.cholesky(gram_matrix)
    ortho = jax.scipy.linalg.solve_triangular(lower_factor, projected.T, lower=True).T
    right_product = lax.dot_general(ortho.astype(jnp.float32), summed.astype(jnp.float32), (((0,), (0,)), ((), ())), precision=highest, preferred_element_type=jnp.float32)
    inverse = lax.rsqrt(lax.optimization_barrier(jnp.mean(right_product * right_product, axis=1, keepdims=True)) + epsilon)
    new_factor = right_product * inverse
    new_momentum = summed - (1.0 - momentum_keep) * jnp.dot(ortho.astype(jnp.float32), right_product.astype(jnp.float32), precision=highest, preferred_element_type=jnp.float32)
    step_scale = learn_rate * math.sqrt(MDIM / RANK)
    new_weight = (1.0 - learn_rate * weight_decay) * weight - step_scale * jnp.dot(ortho.astype(jnp.float32), new_factor.astype(jnp.float32), precision=highest, preferred_element_type=jnp.float32)
    return (new_momentum, new_weight, new_factor)
```

```python
import math

import jax
import jax.numpy as jnp
from jax import lax
from jax.sharding import PartitionSpec as P

MDIM = 7168
NDIM = 18432
RANK = 256

epsilon = 1e-06
momentum_keep = 0.95
learn_rate = 0.3
weight_decay = 0.1

HIGHEST = lax.Precision.HIGHEST

ROWS = 16
DEPTH = 8
Z_GROUPS = [[2 * z + core for z in range(DEPTH)] for core in range(2)]
CORE_SWAP = [(i, i ^ 1) for i in range(2 * DEPTH)]


def z_pairs(partner):
    return [(2 * z + core, 2 * partner[z] + core) for z in range(DEPTH) for core in range(2)]


Z_BUTTERFLY = (
    z_pairs([1, 0, 3, 2, 5, 4, 7, 6]),
    z_pairs([7, 2, 1, 4, 3, 6, 5, 0]),
    z_pairs([3, 6, 5, 0, 7, 2, 1, 4]),
)


def product(a, b, contract):
    return lax.dot_general(
        a, b, (contract, ((), ())), precision=HIGHEST, preferred_element_type=jnp.float32
    )


def gather_over_row(block):
    copies = jnp.broadcast_to(block[None], (ROWS,) + block.shape)
    return lax.all_to_all(copies, "row", 0, 0).reshape((ROWS * block.shape[0],) + block.shape[1:])


def sum_over_row(whole):
    parts = whole.reshape((ROWS, whole.shape[0] // ROWS) + whole.shape[1:])
    return jnp.sum(lax.all_to_all(parts, "row", 0, 0), axis=0)


def sum_over_col(whole):
    core = lax.axis_index("col") % 2
    half = whole.shape[0] // 2
    kept = lax.dynamic_slice_in_dim(whole, core * half, half, 0)
    given = lax.dynamic_slice_in_dim(whole, (1 - core) * half, half, 0)
    chip = kept + lax.ppermute(given, "col", CORE_SWAP)
    parts = chip.reshape((DEPTH, half // DEPTH) + whole.shape[1:])
    part = jnp.sum(lax.all_to_all(parts, "col", 0, 0, axis_index_groups=Z_GROUPS), axis=0)
    copies = jnp.broadcast_to(part[None], (DEPTH,) + part.shape)
    mine = lax.all_to_all(copies, "col", 0, 0, axis_index_groups=Z_GROUPS).reshape(chip.shape)
    other = lax.ppermute(mine, "col", CORE_SWAP)
    return jnp.where(
        core == 0, jnp.concatenate([mine, other], 0), jnp.concatenate([other, mine], 0)
    )


def sum_small_over_col(value):
    value = value + lax.ppermute(value, "col", CORE_SWAP)
    for pairs in Z_BUTTERFLY:
        value = value + lax.ppermute(value, "col", pairs)
    return value


def per_device(momentum, gradient, weight, right_factor):
    summed = momentum + gradient.astype(jnp.float32)
    right_all = gather_over_row(right_factor)
    partial_value = product(right_all, summed, ((1,), (1,)))
    projected = sum_over_col(partial_value)
    local_gram = product(projected, projected, ((1,), (1,)))
    local_cross = product(projected, summed, ((1,), (0,)))
    both = gather_over_row(sum_over_row(jnp.concatenate([local_cross, local_gram], axis=1)))
    cross, gram_matrix = both[:, : summed.shape[1]], both[:, summed.shape[1] :]
    lower_factor = jnp.linalg.cholesky(gram_matrix)
    lower_inverse = jax.scipy.linalg.solve_triangular(
        lower_factor, jnp.eye(RANK, dtype=jnp.float32), lower=True
    )
    right_product = product(lower_inverse, cross, ((1,), (0,)))
    squares = sum_small_over_col(jnp.sum(right_product * right_product, axis=1)[None])[0]
    ortho_t = product(lower_inverse, projected, ((1,), (0,)))
    momentum_delta = product(ortho_t, right_product, ((0,), (0,)))
    new_momentum = summed - (1.0 - momentum_keep) * momentum_delta
    inverse = lax.rsqrt(squares / NDIM + epsilon)
    factor_all = right_product * inverse[:, None]
    weight_delta = product(ortho_t, factor_all, ((0,), (0,)))
    step_scale = learn_rate * math.sqrt(MDIM / RANK)
    band_rows = right_factor.shape[0]
    new_factor = lax.dynamic_slice_in_dim(
        factor_all, lax.axis_index("row") * band_rows, band_rows, 0
    )
    new_weight = (1.0 - learn_rate * weight_decay) * weight - step_scale * weight_delta
    return (new_momentum, new_weight, new_factor)


def solution(mesh):
    in_specs = (P("row", "col"), P("row", "col"), P("row", "col"), P("row", "col"))
    out_specs = (P("row", "col"), P("row", "col"), P("row", "col"))
    return jax.shard_map(
        per_device, mesh=mesh, in_specs=in_specs, out_specs=out_specs, check_vma=False
    )
```

```python
import math

import jax
import jax.numpy as jnp
from jax import lax
from jax.experimental import pallas as pl
from jax.experimental.pallas import tpu as pltpu
from jax.sharding import PartitionSpec as P

MDIM = 7168
NDIM = 18432
RANK = 256

epsilon = 1e-06
momentum_keep = 0.95
learn_rate = 0.3
weight_decay = 0.1

HIGHEST = lax.Precision.HIGHEST

ROWS = 16
DEPTH = 8
Z_GROUPS = [[2 * z + core for z in range(DEPTH)] for core in range(2)]
CORE_SWAP = [(i, i ^ 1) for i in range(2 * DEPTH)]


def z_pairs(partner):
    return [(2 * z + core, 2 * partner[z] + core) for z in range(DEPTH) for core in range(2)]


Z_BUTTERFLY = (
    z_pairs([1, 0, 3, 2, 5, 4, 7, 6]),
    z_pairs([7, 2, 1, 4, 3, 6, 5, 0]),
    z_pairs([3, 6, 5, 0, 7, 2, 1, 4]),
)


def product(a, b, contract):
    return lax.dot_general(
        a, b, (contract, ((), ())), precision=HIGHEST, preferred_element_type=jnp.float32
    )


def gather_over_row(block):
    copies = jnp.broadcast_to(block[None], (ROWS,) + block.shape)
    return lax.all_to_all(copies, "row", 0, 0).reshape((ROWS * block.shape[0],) + block.shape[1:])


def sum_over_row(whole):
    parts = whole.reshape((ROWS, whole.shape[0] // ROWS) + whole.shape[1:])
    return jnp.sum(lax.all_to_all(parts, "row", 0, 0), axis=0)


def sum_over_col(whole):
    core = lax.axis_index("col") % 2
    half = whole.shape[0] // 2
    kept = lax.dynamic_slice_in_dim(whole, core * half, half, 0)
    given = lax.dynamic_slice_in_dim(whole, (1 - core) * half, half, 0)
    chip = kept + lax.ppermute(given, "col", CORE_SWAP)
    parts = chip.reshape((DEPTH, half // DEPTH) + whole.shape[1:])
    part = jnp.sum(lax.all_to_all(parts, "col", 0, 0, axis_index_groups=Z_GROUPS), axis=0)
    copies = jnp.broadcast_to(part[None], (DEPTH,) + part.shape)
    mine = lax.all_to_all(copies, "col", 0, 0, axis_index_groups=Z_GROUPS).reshape(chip.shape)
    other = lax.ppermute(mine, "col", CORE_SWAP)
    return jnp.where(
        core == 0, jnp.concatenate([mine, other], 0), jnp.concatenate([other, mine], 0)
    )


def sum_small_over_col(value):
    value = value + lax.ppermute(value, "col", CORE_SWAP)
    for pairs in Z_BUTTERFLY:
        value = value + lax.ppermute(value, "col", pairs)
    return value


BAND = 32
SUB = 8
LANES = 128


def inverse_factor_kernel(gram_ref, out_ref, work):
    n = out_ref.shape[0]
    groups, tiles = BAND // SUB, n // LANES
    row_of = lax.broadcasted_iota(jnp.int32, (SUB, LANES), 0)
    work[...] = gram_ref[...]
    for start in range(0, n, BAND):
        columns = [
            [
                jnp.broadcast_to(
                    work[start + SUB * g : start + SUB * (g + 1), start + j : start + j + 1],
                    (SUB, LANES),
                )
                if g >= j // SUB
                else None
                for g in range(groups)
            ]
            for j in range(BAND)
        ]
        place = lax.broadcasted_iota(jnp.int32, (BAND, n), 1) - start
        identity = (place == lax.broadcasted_iota(jnp.int32, (BAND, n), 0)).astype(jnp.float32)
        band = jnp.where((place >= 0) & (place < BAND), identity, work[start : start + BAND, :])
        rows = [
            [band[SUB * g : SUB * (g + 1), LANES * t : LANES * (t + 1)] for t in range(tiles)]
            for g in range(groups)
        ]
        for k in range(BAND):
            own, at = divmod(k, SUB)
            pivot = jnp.broadcast_to(columns[k][own][at : at + 1, :], (SUB, LANES))
            root = lax.rsqrt(pivot)
            reciprocal = root * root
            for j in range(k + 1, BAND):
                g0, at_j = divmod(j, SUB)
                scale = jnp.broadcast_to(columns[k][g0][at_j : at_j + 1, :], (SUB, LANES)) * reciprocal
                for g in range(g0, groups):
                    columns[j][g] = columns[j][g] - columns[k][g] * scale
            row = [jnp.broadcast_to(rows[own][t][at : at + 1, :], (SUB, LANES)) for t in range(tiles)]
            scaled = [value * reciprocal for value in row]
            for g in range(own, groups):
                column = columns[k][g]
                if g == own:
                    column = jnp.where(row_of > at, column, 0.0)
                for t in range(tiles):
                    updated = rows[g][t] - column * scaled[t]
                    if g == own:
                        updated = jnp.where(row_of == at, row[t] * root, updated)
                    rows[g][t] = updated
        for g in range(groups):
            for t in range(tiles):
                work[start + SUB * g : start + SUB * (g + 1), LANES * t : LANES * (t + 1)] = rows[g][t]
        below = n - start - BAND
        if below:
            update = lax.dot_general(
                work[start : start + BAND, start + BAND :],
                work[start : start + BAND, :],
                (((0,), (0,)), ((), ())),
                precision=HIGHEST,
                preferred_element_type=jnp.float32,
            )
            place = lax.broadcasted_iota(jnp.int32, (below, n), 1) - start
            old = jnp.where((place >= 0) & (place < BAND), 0.0, work[start + BAND :, :])
            work[start + BAND :, :] = old - update
    row = lax.broadcasted_iota(jnp.int32, (n, n), 0)
    column = lax.broadcasted_iota(jnp.int32, (n, n), 1)
    out_ref[...] = jnp.where(row >= column, work[...], 0.0)


def inverse_factor(gram_and_more):
    n = gram_and_more.shape[0]
    block = pl.BlockSpec((n, n), lambda i: (0, 0))
    return pl.pallas_call(
        inverse_factor_kernel,
        grid=(1,),
        out_shape=jax.ShapeDtypeStruct((n, n), jnp.float32),
        in_specs=[block],
        out_specs=block,
        scratch_shapes=[pltpu.VMEM((n, n), jnp.float32)],
        cost_estimate=pl.CostEstimate(flops=2 * n**3, bytes_accessed=8 * n * n, transcendentals=n),
    )(gram_and_more)


def per_device(momentum, gradient, weight, right_factor):
    summed = momentum + gradient.astype(jnp.float32)
    right_all = gather_over_row(right_factor)
    partial_value = product(right_all, summed, ((1,), (1,)))
    projected = sum_over_col(partial_value)
    local_gram = product(projected, projected, ((1,), (1,)))
    local_cross = product(projected, summed, ((1,), (0,)))
    both = gather_over_row(sum_over_row(jnp.concatenate([local_gram, local_cross], axis=1)))
    lower_inverse = inverse_factor(both)
    cross = both[:, RANK:]
    right_product = product(lower_inverse, cross, ((1,), (0,)))
    squares = sum_small_over_col(jnp.sum(right_product * right_product, axis=1)[None])[0]
    ortho_t = product(lower_inverse, projected, ((1,), (0,)))
    momentum_delta = product(ortho_t, right_product, ((0,), (0,)))
    new_momentum = summed - (1.0 - momentum_keep) * momentum_delta
    inverse = lax.rsqrt(squares / NDIM + epsilon)
    factor_all = right_product * inverse[:, None]
    weight_delta = product(ortho_t, factor_all, ((0,), (0,)))
    step_scale = learn_rate * math.sqrt(MDIM / RANK)
    band_rows = right_factor.shape[0]
    new_factor = lax.dynamic_slice_in_dim(
        factor_all, lax.axis_index("row") * band_rows, band_rows, 0
    )
    new_weight = (1.0 - learn_rate * weight_decay) * weight - step_scale * weight_delta
    return (new_momentum, new_weight, new_factor)


def solution(mesh):
    in_specs = (P("row", "col"), P("row", "col"), P("row", "col"), P("row", "col"))
    out_specs = (P("row", "col"), P("row", "col"), P("row", "col"))
    return jax.shard_map(
        per_device, mesh=mesh, in_specs=in_specs, out_specs=out_specs, check_vma=False
    )
```

```python
import math

import jax
import jax.numpy as jnp
from jax import lax
from jax.experimental import pallas as pl
from jax.experimental.pallas import tpu as pltpu
from jax.sharding import PartitionSpec as P

MDIM = 7168
NDIM = 18432
RANK = 256

epsilon = 1e-06
momentum_keep = 0.95
learn_rate = 0.3
weight_decay = 0.1

HIGHEST = lax.Precision.HIGHEST

ROWS = 16
DEPTH = 8
Z_GROUPS = [[2 * z + core for z in range(DEPTH)] for core in range(2)]
CORE_SWAP = [(i, i ^ 1) for i in range(2 * DEPTH)]


def pairs_on(partner, others, index):
    return [(index(i, j), index(partner[i], j)) for i in range(len(partner)) for j in range(others)]


def z_pairs(partner):
    return pairs_on(partner, 2, lambda z, core: 2 * z + core)


Z_BUTTERFLY = (
    z_pairs([1, 0, 3, 2, 5, 4, 7, 6]),
    z_pairs([7, 2, 1, 4, 3, 6, 5, 0]),
    z_pairs([3, 6, 5, 0, 7, 2, 1, 4]),
)

def product(a, b, contract, precision=HIGHEST):
    return lax.dot_general(
        a, b, (contract, ((), ())), precision=precision, preferred_element_type=jnp.float32
    )


def gather_over_row(block):
    copies = jnp.broadcast_to(block[None], (ROWS,) + block.shape)
    return lax.all_to_all(copies, "row", 0, 0).reshape((ROWS * block.shape[0],) + block.shape[1:])


def sum_over_row(whole):
    parts = whole.reshape((ROWS, whole.shape[0] // ROWS) + whole.shape[1:])
    return jnp.sum(lax.all_to_all(parts, "row", 0, 0), axis=0)


def sum_over_col(whole):
    core = lax.axis_index("col") % 2
    rows, columns = whole.shape
    half = columns // 2
    kept = lax.dynamic_slice_in_dim(whole, core * half, half, 1)
    given = lax.dynamic_slice_in_dim(whole, (1 - core) * half, half, 1)
    chip = kept + lax.ppermute(given, "col", CORE_SWAP)
    parts = chip.reshape(DEPTH, rows // DEPTH, half)
    part = jnp.sum(lax.all_to_all(parts, "col", 0, 0, axis_index_groups=Z_GROUPS), axis=0)
    copies = jnp.broadcast_to(part[None], (DEPTH,) + part.shape)
    mine = lax.all_to_all(copies, "col", 0, 0, axis_index_groups=Z_GROUPS).reshape(chip.shape)
    return in_order(core == 0, mine, lax.ppermute(mine, "col", CORE_SWAP), 1)


def in_order(first, mine, other, axis=0):
    return jnp.where(
        first, jnp.concatenate([mine, other], axis), jnp.concatenate([other, mine], axis)
    )


def band_index():
    place = lax.axis_index("col")
    return place % 2 * 4 + place // 2 % 4


def gather_bands(band, other):
    place = lax.axis_index("col")
    core, z = place % 2, place // 2
    received, other = lax.optimization_barrier((lax.ppermute(band, "col", Z_BUTTERFLY[0]), other))
    mine = in_order(z % 2 == 0, band, received)
    mine = in_order(z // 2 % 2 == 0, mine, lax.ppermute(mine, "col", Z_BUTTERFLY[1]))
    return in_order(core == 0, mine, lax.ppermute(mine, "col", CORE_SWAP)), other


def sum_small_over_col(value):
    value = value + lax.ppermute(value, "col", CORE_SWAP)
    for pairs in Z_BUTTERFLY:
        value = value + lax.ppermute(value, "col", pairs)
    return value


BAND = 32
SUB = 8
LANES = 128


def inverse_factor_kernel(gram_ref, out_ref, work):
    n = out_ref.shape[0]
    groups, tiles = BAND // SUB, n // LANES
    row_of = lax.broadcasted_iota(jnp.int32, (SUB, LANES), 0)
    work[...] = gram_ref[...]
    for start in range(0, n, BAND):
        columns = [
            [
                jnp.broadcast_to(
                    work[start + SUB * g : start + SUB * (g + 1), start + j : start + j + 1],
                    (SUB, LANES),
                )
                if g >= j // SUB
                else None
                for g in range(groups)
            ]
            for j in range(BAND)
        ]
        place = lax.broadcasted_iota(jnp.int32, (BAND, n), 1) - start
        identity = (place == lax.broadcasted_iota(jnp.int32, (BAND, n), 0)).astype(jnp.float32)
        band = jnp.where((place >= 0) & (place < BAND), identity, work[start : start + BAND, :])
        rows = [
            [band[SUB * g : SUB * (g + 1), LANES * t : LANES * (t + 1)] for t in range(tiles)]
            for g in range(groups)
        ]
        for k in range(BAND):
            own, at = divmod(k, SUB)
            pivot = jnp.broadcast_to(columns[k][own][at : at + 1, :], (SUB, LANES))
            root = lax.rsqrt(pivot)
            reciprocal = root * root
            for j in range(k + 1, BAND):
                g0, at_j = divmod(j, SUB)
                scale = jnp.broadcast_to(columns[k][g0][at_j : at_j + 1, :], (SUB, LANES)) * reciprocal
                for g in range(g0, groups):
                    columns[j][g] = columns[j][g] - columns[k][g] * scale
            row = [jnp.broadcast_to(rows[own][t][at : at + 1, :], (SUB, LANES)) for t in range(tiles)]
            scaled = [value * reciprocal for value in row]
            for g in range(own, groups):
                column = columns[k][g]
                if g == own:
                    column = jnp.where(row_of > at, column, 0.0)
                for t in range(tiles):
                    updated = rows[g][t] - column * scaled[t]
                    if g == own:
                        updated = jnp.where(row_of == at, row[t] * root, updated)
                    rows[g][t] = updated
        for g in range(groups):
            for t in range(tiles):
                work[start + SUB * g : start + SUB * (g + 1), LANES * t : LANES * (t + 1)] = rows[g][t]
        below = n - start - BAND
        if below:
            update = lax.dot_general(
                work[start : start + BAND, start + BAND :],
                work[start : start + BAND, :],
                (((0,), (0,)), ((), ())),
                precision=HIGHEST,
                preferred_element_type=jnp.float32,
            )
            place = lax.broadcasted_iota(jnp.int32, (below, n), 1) - start
            old = jnp.where((place >= 0) & (place < BAND), 0.0, work[start + BAND :, :])
            work[start + BAND :, :] = old - update
    row = lax.broadcasted_iota(jnp.int32, (n, n), 0)
    column = lax.broadcasted_iota(jnp.int32, (n, n), 1)
    out_ref[...] = jnp.where(row >= column, work[...], 0.0)


def inverse_factor(gram_and_more):
    n = gram_and_more.shape[0]
    block = pl.BlockSpec((n, n), lambda i: (0, 0))
    return pl.pallas_call(
        inverse_factor_kernel,
        grid=(1,),
        out_shape=jax.ShapeDtypeStruct((n, n), jnp.float32),
        in_specs=[block],
        out_specs=block,
        scratch_shapes=[pltpu.VMEM((n, n), jnp.float32)],
        cost_estimate=pl.CostEstimate(flops=2 * n**3, bytes_accessed=8 * n * n, transcendentals=n),
    )(gram_and_more)


def per_device(momentum, gradient, weight, right_factor):
    summed = momentum + gradient.astype(jnp.float32)
    right_all = gather_over_row(right_factor)
    projected = sum_over_col(product(summed, right_all, ((1,), (1,))))
    local_cross = product(projected, summed, ((0,), (0,)))
    local_gram = product(projected, projected, ((0,), (0,)))
    rows, band = RANK // ROWS, RANK // 8
    at = band_index() * band
    band_parts = [lax.dynamic_slice_in_dim(local_gram, at + i, rows, 0) for i in range(0, band, rows)]
    bands = jnp.broadcast_to(jnp.concatenate(band_parts, 1)[None], (ROWS, rows, RANK * band // rows))
    parts = jnp.concatenate([local_cross.reshape(ROWS, rows, -1), bands], axis=2)
    taken = lax.all_to_all(parts, "row", 0, 0)
    columns = summed.shape[1]
    gram_band = jnp.sum(taken[:, :, columns:], axis=0)
    gram_band = jnp.concatenate(
        [gram_band[:, i * RANK : (i + 1) * RANK] for i in range(band // rows)], 0
    )
    gram_matrix, cross_part = gather_bands(gram_band, jnp.sum(taken[:, :, :columns], axis=0))
    cross = gather_over_row(cross_part)
    lower_inverse = inverse_factor(gram_matrix)
    right_product = product(lower_inverse, cross, ((1,), (0,)))
    squares = sum_small_over_col(jnp.sum(right_product * right_product, axis=1)[None])[0]
    ortho = product(projected, lower_inverse, ((1,), (1,)))
    momentum_delta = product(ortho, right_product, ((1,), (0,)), lax.Precision.HIGH)
    new_momentum = summed - (1.0 - momentum_keep) * momentum_delta
    inverse = lax.rsqrt(squares / NDIM + epsilon)
    factor_all = right_product * inverse[:, None]
    weight_delta = product(ortho, factor_all, ((1,), (0,)), lax.Precision.HIGH)
    step_scale = learn_rate * math.sqrt(MDIM / RANK)
    band_rows = right_factor.shape[0]
    new_factor = lax.dynamic_slice_in_dim(
        factor_all, lax.axis_index("row") * band_rows, band_rows, 0
    )
    new_weight = (1.0 - learn_rate * weight_decay) * weight - step_scale * weight_delta
    return (new_momentum, new_weight, new_factor)


def solution(mesh):
    in_specs = (P("row", "col"), P("row", "col"), P("row", "col"), P("row", "col"))
    out_specs = (P("row", "col"), P("row", "col"), P("row", "col"))
    return jax.shard_map(
        per_device, mesh=mesh, in_specs=in_specs, out_specs=out_specs, check_vma=False
    )
```

```python
import math

import jax
import jax.numpy as jnp
from jax import lax
from jax.experimental import pallas as pl
from jax.experimental.pallas import tpu as pltpu
from jax.sharding import PartitionSpec as P

MDIM = 7168
NDIM = 18432
RANK = 256

epsilon = 1e-06
momentum_keep = 0.95
learn_rate = 0.3
weight_decay = 0.1

HIGHEST = lax.Precision.HIGHEST

ROWS = 16
DEPTH = 8
Z_GROUPS = [[2 * z + core for z in range(DEPTH)] for core in range(2)]
CORE_SWAP = [(i, i ^ 1) for i in range(2 * DEPTH)]


def pairs_on(partner, others, index):
    return [(index(i, j), index(partner[i], j)) for i in range(len(partner)) for j in range(others)]


def z_pairs(partner):
    return pairs_on(partner, 2, lambda z, core: 2 * z + core)


Z_BUTTERFLY = (
    z_pairs([1, 0, 3, 2, 5, 4, 7, 6]),
    z_pairs([7, 2, 1, 4, 3, 6, 5, 0]),
    z_pairs([3, 6, 5, 0, 7, 2, 1, 4]),
)

def product(a, b, contract, precision=HIGHEST):
    return lax.dot_general(
        a, b, (contract, ((), ())), precision=precision, preferred_element_type=jnp.float32
    )


def gather_over_row(copies):
    block = copies[0]
    return lax.all_to_all(copies, "row", 0, 0).reshape((ROWS * block.shape[0],) + block.shape[1:])


def sum_over_row(whole):
    parts = whole.reshape((ROWS, whole.shape[0] // ROWS) + whole.shape[1:])
    return jnp.sum(lax.all_to_all(parts, "row", 0, 0), axis=0)


def sum_over_col(whole):
    core = lax.axis_index("col") % 2
    rows, columns = whole.shape
    half = columns // 2
    kept = lax.dynamic_slice_in_dim(whole, core * half, half, 1)
    given = lax.dynamic_slice_in_dim(whole, (1 - core) * half, half, 1)
    chip = kept + lax.ppermute(given, "col", CORE_SWAP)
    parts = chip.reshape(DEPTH, rows // DEPTH, half)
    part = jnp.sum(lax.all_to_all(parts, "col", 0, 0, axis_index_groups=Z_GROUPS), axis=0)
    copies = jnp.broadcast_to(part[None], (DEPTH,) + part.shape)
    mine = lax.all_to_all(copies, "col", 0, 0, axis_index_groups=Z_GROUPS).reshape(chip.shape)
    return in_order(core == 0, mine, lax.ppermute(mine, "col", CORE_SWAP), 1)


def in_order(first, mine, other, axis=0):
    return jnp.where(
        first, jnp.concatenate([mine, other], axis), jnp.concatenate([other, mine], axis)
    )


def band_index():
    place = lax.axis_index("col")
    return place % 2 * 4 + place // 2 % 4


def gather_bands(band, other):
    place = lax.axis_index("col")
    core, z = place % 2, place // 2
    band, other = lax.optimization_barrier((band, other))
    received = lax.ppermute(band, "col", Z_BUTTERFLY[0])
    mine = in_order(z % 2 == 0, band, received)
    mine = in_order(z // 2 % 2 == 0, mine, lax.ppermute(mine, "col", Z_BUTTERFLY[1]))
    return in_order(core == 0, mine, lax.ppermute(mine, "col", CORE_SWAP)), other


def sum_small_over_col(value):
    value = value + lax.ppermute(value, "col", CORE_SWAP)
    copies = jnp.broadcast_to(value[None], (DEPTH,) + value.shape)
    return jnp.sum(lax.all_to_all(copies, "col", 0, 0, axis_index_groups=Z_GROUPS), axis=0)


BAND = 32
SUB = 8
LANES = 128


def inverse_factor_kernel(gram_ref, out_ref, work):
    n = out_ref.shape[0]
    groups, tiles = BAND // SUB, n // LANES
    row_of = lax.broadcasted_iota(jnp.int32, (SUB, LANES), 0)
    half = n // 2
    work[:half, :] = gram_ref[:, :n]
    work[half:, :half] = jnp.zeros((n - half, half), jnp.float32)
    work[half:, half:] = gram_ref[:, n:]
    for start in range(0, n, BAND):
        columns = [
            [
                jnp.broadcast_to(
                    work[start + SUB * g : start + SUB * (g + 1), start + j : start + j + 1],
                    (SUB, LANES),
                )
                if g >= j // SUB
                else None
                for g in range(groups)
            ]
            for j in range(BAND)
        ]
        place = lax.broadcasted_iota(jnp.int32, (BAND, n), 1) - start
        identity = (place == lax.broadcasted_iota(jnp.int32, (BAND, n), 0)).astype(jnp.float32)
        band = jnp.where((place >= 0) & (place < BAND), identity, work[start : start + BAND, :])
        rows = [
            [band[SUB * g : SUB * (g + 1), LANES * t : LANES * (t + 1)] for t in range(tiles)]
            for g in range(groups)
        ]
        for k in range(BAND):
            own, at = divmod(k, SUB)
            pivot = jnp.broadcast_to(columns[k][own][at : at + 1, :], (SUB, LANES))
            root = lax.rsqrt(pivot)
            reciprocal = root * root
            for j in range(k + 1, BAND):
                g0, at_j = divmod(j, SUB)
                scale = jnp.broadcast_to(columns[k][g0][at_j : at_j + 1, :], (SUB, LANES)) * reciprocal
                for g in range(g0, groups):
                    columns[j][g] = columns[j][g] - columns[k][g] * scale
            row = [jnp.broadcast_to(rows[own][t][at : at + 1, :], (SUB, LANES)) for t in range(tiles)]
            scaled = [value * reciprocal for value in row]
            for g in range(own, groups):
                column = columns[k][g]
                if g == own:
                    column = jnp.where(row_of > at, column, 0.0)
                for t in range(tiles):
                    updated = rows[g][t] - column * scaled[t]
                    if g == own:
                        updated = jnp.where(row_of == at, row[t] * root, updated)
                    rows[g][t] = updated
        for g in range(groups):
            for t in range(tiles):
                work[start + SUB * g : start + SUB * (g + 1), LANES * t : LANES * (t + 1)] = rows[g][t]
        below = n - start - BAND
        if below:
            value = work[start : start + BAND, :]
            first = value.astype(jnp.bfloat16)
            rest = value - first.astype(jnp.float32)
            second = rest.astype(jnp.bfloat16)
            third = (rest - second.astype(jnp.float32)).astype(jnp.bfloat16)
            left = jnp.concatenate([first, first, second, second, first, third], 0)
            right = jnp.concatenate([first, second, first, second, third, first], 0)
            update = lax.dot_general(
                left[:, start + BAND :],
                right,
                (((0,), (0,)), ((), ())),
                preferred_element_type=jnp.float32,
            )
            place = lax.broadcasted_iota(jnp.int32, (below, n), 1) - start
            old = jnp.where((place >= 0) & (place < BAND), 0.0, work[start + BAND :, :])
            work[start + BAND :, :] = old - update
    row = lax.broadcasted_iota(jnp.int32, (n, n), 0)
    column = lax.broadcasted_iota(jnp.int32, (n, n), 1)
    out_ref[...] = jnp.where(row >= column, work[...], 0.0)


def inverse_factor(packed):
    n = 2 * packed.shape[0]
    return pl.pallas_call(
        inverse_factor_kernel,
        out_shape=jax.ShapeDtypeStruct((n, n), jnp.float32),
        in_specs=[pl.BlockSpec(memory_space=pltpu.VMEM)],
        out_specs=pl.BlockSpec(memory_space=pltpu.VMEM),
        scratch_shapes=[pltpu.VMEM((n, n), jnp.float32)],
        compiler_params=pltpu.CompilerParams(vmem_limit_bytes=6 * 2**20),
        cost_estimate=pl.CostEstimate(flops=2 * n**3, bytes_accessed=8 * n * n, transcendentals=n),
    )(packed)


def right_product_kernel(inverse_ref, cross_ref, out_ref, squares_ref, total):
    step = pl.program_id(0)
    value = product(inverse_ref[...], cross_ref[...], ((1,), (0,)))
    out_ref[...] = value
    squared = value * value
    tiles = [squared[:, LANES * t : LANES * (t + 1)] for t in range(value.shape[1] // LANES)]

    @pl.when(step == 0)
    def _():
        total[...] = sum(tiles)

    @pl.when(step > 0)
    def _():
        total[...] += sum(tiles)

    @pl.when(step == pl.num_programs(0) - 1)
    def _():
        squares_ref[...] = jnp.sum(total[...].T, axis=0, keepdims=True)


def right_product_and_squares(inverse, cross):
    rank, columns = cross.shape
    block = 3 * LANES
    whole = pl.BlockSpec((rank, rank), lambda i: (0, 0))
    strip = pl.BlockSpec((rank, block), lambda i: (0, i))
    return pl.pallas_call(
        right_product_kernel,
        grid=(columns // block,),
        out_shape=(
            jax.ShapeDtypeStruct(cross.shape, jnp.float32),
            jax.ShapeDtypeStruct((1, rank), jnp.float32),
        ),
        in_specs=[whole, strip],
        out_specs=(strip, pl.BlockSpec((1, rank), lambda i: (0, 0))),
        scratch_shapes=[pltpu.VMEM((rank, LANES), jnp.float32)],
        compiler_params=pltpu.CompilerParams(vmem_limit_bytes=8 * 2**20),
        cost_estimate=pl.CostEstimate(
            flops=12 * rank * rank * columns, bytes_accessed=8 * cross.size, transcendentals=0
        ),
    )(inverse, cross)


def repeat_kernel(block_ref, out_ref, semaphores):
    copies = [
        pltpu.make_async_copy(block_ref, out_ref.at[i], semaphores.at[i])
        for i in range(out_ref.shape[0])
    ]
    for copy in copies:
        copy.start()
    for copy in copies:
        copy.wait()


def repeat(block, times):
    return pl.pallas_call(
        repeat_kernel,
        out_shape=jax.ShapeDtypeStruct((times,) + block.shape, block.dtype),
        in_specs=[pl.BlockSpec(memory_space=pl.ANY)],
        out_specs=pl.BlockSpec(memory_space=pl.ANY),
        scratch_shapes=[pltpu.SemaphoreType.DMA((times,))],
        compiler_params=pltpu.CompilerParams(vmem_limit_bytes=2**20),
        cost_estimate=pl.CostEstimate(
            flops=0, bytes_accessed=8 * times * block.size, transcendentals=0
        ),
    )(block)


def per_device(momentum, gradient, weight, right_factor):
    summed = momentum + gradient.astype(jnp.float32)
    right_all = gather_over_row(repeat(right_factor, ROWS))
    projected = sum_over_col(product(summed, right_all, ((1,), (1,))))
    local_cross = product(projected, summed, ((0,), (0,)))
    half = RANK // 2
    local_gram = product(projected, projected, ((0,), (0,)))
    rows, columns = RANK // ROWS, summed.shape[1]
    at = band_index() * rows
    band = jnp.concatenate(
        [
            lax.dynamic_slice_in_dim(local_gram, at, rows, 0),
            lax.dynamic_slice_in_dim(local_gram, at + half, rows, 0)[:, half:],
        ],
        1,
    )
    bands = jnp.broadcast_to(band[None], (ROWS,) + band.shape)
    parts = jnp.concatenate([local_cross.reshape(ROWS, rows, -1), bands], axis=2)
    taken = lax.all_to_all(parts, "row", 0, 0)
    gram_band = jnp.sum(taken[:, :, columns:], axis=0)
    packed, cross_part = gather_bands(gram_band, jnp.sum(taken[:, :, :columns], axis=0))
    cross = gather_over_row(jnp.broadcast_to(cross_part[None], (ROWS,) + cross_part.shape))
    lower_inverse = inverse_factor(packed)
    right_product, squares = right_product_and_squares(lower_inverse, cross)
    squares = sum_small_over_col(squares)[0]
    ortho = product(projected, lower_inverse, ((1,), (1,)))
    momentum_delta = product(ortho, right_product, ((1,), (0,)), lax.Precision.HIGH)
    new_momentum = summed - (1.0 - momentum_keep) * momentum_delta
    inverse = lax.rsqrt(squares / NDIM + epsilon)
    factor_all = right_product * inverse[:, None]
    weight_delta = product(ortho, factor_all, ((1,), (0,)), lax.Precision.HIGH)
    step_scale = learn_rate * math.sqrt(MDIM / RANK)
    band_rows = right_factor.shape[0]
    new_factor = lax.dynamic_slice_in_dim(
        factor_all, lax.axis_index("row") * band_rows, band_rows, 0
    )
    new_weight = (1.0 - learn_rate * weight_decay) * weight - step_scale * weight_delta
    return (new_momentum, new_weight, new_factor)


def solution(mesh):
    in_specs = (P("row", "col"), P("row", "col"), P("row", "col"), P("row", "col"))
    out_specs = (P("row", "col"), P("row", "col"), P("row", "col"))
    return jax.shard_map(
        per_device, mesh=mesh, in_specs=in_specs, out_specs=out_specs, check_vma=False
    )
```

```python
import math

import jax
import jax.numpy as jnp
from jax import lax
from jax.experimental import pallas as pl
from jax.experimental.pallas import tpu as pltpu
from jax.sharding import PartitionSpec as P

MDIM = 7168
NDIM = 18432
RANK = 256

epsilon = 1e-06
momentum_keep = 0.95
learn_rate = 0.3
weight_decay = 0.1

HIGHEST = lax.Precision.HIGHEST

ROWS = 16
DEPTH = 8
Z_GROUPS = [[2 * z + core for z in range(DEPTH)] for core in range(2)]
CORE_SWAP = [(i, i ^ 1) for i in range(2 * DEPTH)]


def pairs_on(partner, others, index):
    return [(index(i, j), index(partner[i], j)) for i in range(len(partner)) for j in range(others)]


def z_pairs(partner):
    return pairs_on(partner, 2, lambda z, core: 2 * z + core)


Z_BUTTERFLY = (
    z_pairs([1, 0, 3, 2, 5, 4, 7, 6]),
    z_pairs([7, 2, 1, 4, 3, 6, 5, 0]),
    z_pairs([3, 6, 5, 0, 7, 2, 1, 4]),
)

def product(a, b, contract, precision=HIGHEST):
    return lax.dot_general(
        a, b, (contract, ((), ())), precision=precision, preferred_element_type=jnp.float32
    )


def gather_over_row(copies):
    block = copies[0]
    return lax.all_to_all(copies, "row", 0, 0).reshape((ROWS * block.shape[0],) + block.shape[1:])


def sum_over_row(whole):
    parts = whole.reshape((ROWS, whole.shape[0] // ROWS) + whole.shape[1:])
    return jnp.sum(lax.all_to_all(parts, "row", 0, 0), axis=0)


def sum_over_col(whole):
    core = lax.axis_index("col") % 2
    rows, columns = whole.shape
    half = columns // 2
    kept = lax.dynamic_slice_in_dim(whole, core * half, half, 1)
    given = lax.dynamic_slice_in_dim(whole, (1 - core) * half, half, 1)
    chip = kept + lax.ppermute(given, "col", CORE_SWAP)
    parts = chip.reshape(DEPTH, rows // DEPTH, half)
    part = jnp.sum(lax.all_to_all(parts, "col", 0, 0, axis_index_groups=Z_GROUPS), axis=0)
    copies = jnp.broadcast_to(part[None], (DEPTH,) + part.shape)
    mine = lax.all_to_all(copies, "col", 0, 0, axis_index_groups=Z_GROUPS).reshape(chip.shape)
    return in_order(core == 0, mine, lax.ppermute(mine, "col", CORE_SWAP), 1)


def in_order(first, mine, other, axis=0):
    return jnp.where(
        first, jnp.concatenate([mine, other], axis), jnp.concatenate([other, mine], axis)
    )


def band_index():
    place = lax.axis_index("col")
    return place % 2 * 4 + place // 2 % 4


def gather_bands(band, other):
    place = lax.axis_index("col")
    core, z = place % 2, place // 2
    band, other = lax.optimization_barrier((band, other))
    received = lax.ppermute(band, "col", Z_BUTTERFLY[0])
    mine = in_order(z % 2 == 0, band, received)
    mine = in_order(z // 2 % 2 == 0, mine, lax.ppermute(mine, "col", Z_BUTTERFLY[1]))
    return in_order(core == 0, mine, lax.ppermute(mine, "col", CORE_SWAP)), other


def sum_small_over_col(value):
    value = value + lax.ppermute(value, "col", CORE_SWAP)
    copies = jnp.broadcast_to(value[None], (DEPTH,) + value.shape)
    return jnp.sum(lax.all_to_all(copies, "col", 0, 0, axis_index_groups=Z_GROUPS), axis=0)


BAND = 32
SUB = 8
LANES = 128


def inverse_factor_kernel(gram_ref, out_ref, work):
    n = out_ref.shape[0]
    groups, tiles = BAND // SUB, n // LANES
    row_of = lax.broadcasted_iota(jnp.int32, (SUB, LANES), 0)
    half = n // 2
    work[:half, :] = gram_ref[:, :n]
    work[half:, :half] = jnp.zeros((n - half, half), jnp.float32)
    work[half:, half:] = gram_ref[:, n:]
    for start in range(0, n, BAND):
        columns = [
            [
                jnp.broadcast_to(
                    work[start + SUB * g : start + SUB * (g + 1), start + j : start + j + 1],
                    (SUB, LANES),
                )
                if g >= j // SUB
                else None
                for g in range(groups)
            ]
            for j in range(BAND)
        ]
        place = lax.broadcasted_iota(jnp.int32, (BAND, n), 1) - start
        identity = (place == lax.broadcasted_iota(jnp.int32, (BAND, n), 0)).astype(jnp.float32)
        band = jnp.where((place >= 0) & (place < BAND), identity, work[start : start + BAND, :])
        rows = [
            [band[SUB * g : SUB * (g + 1), LANES * t : LANES * (t + 1)] for t in range(tiles)]
            for g in range(groups)
        ]
        for k in range(BAND):
            own, at = divmod(k, SUB)
            pivot = jnp.broadcast_to(columns[k][own][at : at + 1, :], (SUB, LANES))
            root = lax.rsqrt(pivot)
            reciprocal = root * root
            for j in range(k + 1, BAND):
                g0, at_j = divmod(j, SUB)
                scale = jnp.broadcast_to(columns[k][g0][at_j : at_j + 1, :], (SUB, LANES)) * reciprocal
                for g in range(g0, groups):
                    columns[j][g] = columns[j][g] - columns[k][g] * scale
            row = [jnp.broadcast_to(rows[own][t][at : at + 1, :], (SUB, LANES)) for t in range(tiles)]
            scaled = [value * reciprocal for value in row]
            for g in range(own, groups):
                column = columns[k][g]
                if g == own:
                    column = jnp.where(row_of > at, column, 0.0)
                for t in range(tiles):
                    updated = rows[g][t] - column * scaled[t]
                    if g == own:
                        updated = jnp.where(row_of == at, row[t] * root, updated)
                    rows[g][t] = updated
        for g in range(groups):
            for t in range(tiles):
                work[start + SUB * g : start + SUB * (g + 1), LANES * t : LANES * (t + 1)] = rows[g][t]
        below = n - start - BAND
        if below:
            value = work[start : start + BAND, :]
            first = value.astype(jnp.bfloat16)
            rest = value - first.astype(jnp.float32)
            second = rest.astype(jnp.bfloat16)
            third = (rest - second.astype(jnp.float32)).astype(jnp.bfloat16)
            left = jnp.concatenate([first, first, second, second, first, third], 0)
            right = jnp.concatenate([first, second, first, second, third, first], 0)
            update = lax.dot_general(
                left[:, start + BAND :],
                right,
                (((0,), (0,)), ((), ())),
                preferred_element_type=jnp.float32,
            )
            place = lax.broadcasted_iota(jnp.int32, (below, n), 1) - start
            old = jnp.where((place >= 0) & (place < BAND), 0.0, work[start + BAND :, :])
            work[start + BAND :, :] = old - update
    row = lax.broadcasted_iota(jnp.int32, (n, n), 0)
    column = lax.broadcasted_iota(jnp.int32, (n, n), 1)
    out_ref[...] = jnp.where(row >= column, work[...], 0.0)


def inverse_factor(packed):
    n = 2 * packed.shape[0]
    return pl.pallas_call(
        inverse_factor_kernel,
        out_shape=jax.ShapeDtypeStruct((n, n), jnp.float32),
        in_specs=[pl.BlockSpec(memory_space=pltpu.VMEM)],
        out_specs=pl.BlockSpec(memory_space=pltpu.VMEM),
        scratch_shapes=[pltpu.VMEM((n, n), jnp.float32)],
        compiler_params=pltpu.CompilerParams(vmem_limit_bytes=6 * 2**20),
        cost_estimate=pl.CostEstimate(flops=2 * n**3, bytes_accessed=8 * n * n, transcendentals=n),
    )(packed)


def right_product_kernel(inverse_ref, cross_ref, out_ref, squares_ref, total):
    step = pl.program_id(0)
    value = product(inverse_ref[...], cross_ref[...], ((1,), (0,)))
    out_ref[...] = value
    squared = value * value
    tiles = [squared[:, LANES * t : LANES * (t + 1)] for t in range(value.shape[1] // LANES)]

    @pl.when(step == 0)
    def _():
        total[...] = sum(tiles)

    @pl.when(step > 0)
    def _():
        total[...] += sum(tiles)

    @pl.when(step == pl.num_programs(0) - 1)
    def _():
        squares_ref[...] = jnp.sum(total[...].T, axis=0, keepdims=True)


def right_product_and_squares(inverse, cross):
    rank, columns = cross.shape
    block = 3 * LANES
    whole = pl.BlockSpec((rank, rank), lambda i: (0, 0))
    strip = pl.BlockSpec((rank, block), lambda i: (0, i))
    return pl.pallas_call(
        right_product_kernel,
        grid=(columns // block,),
        out_shape=(
            jax.ShapeDtypeStruct(cross.shape, jnp.float32),
            jax.ShapeDtypeStruct((1, rank), jnp.float32),
        ),
        in_specs=[whole, strip],
        out_specs=(strip, pl.BlockSpec((1, rank), lambda i: (0, 0))),
        scratch_shapes=[pltpu.VMEM((rank, LANES), jnp.float32)],
        compiler_params=pltpu.CompilerParams(vmem_limit_bytes=8 * 2**20),
        cost_estimate=pl.CostEstimate(
            flops=12 * rank * rank * columns, bytes_accessed=8 * cross.size, transcendentals=0
        ),
    )(inverse, cross)


def repeat_kernel(block_ref, out_ref):
    value = block_ref[...]
    for i in range(out_ref.shape[0]):
        out_ref[i] = value


def repeat(block, times):
    return pl.pallas_call(
        repeat_kernel,
        out_shape=jax.ShapeDtypeStruct((times,) + block.shape, block.dtype),
        in_specs=[pl.BlockSpec(memory_space=pltpu.VMEM)],
        out_specs=pl.BlockSpec(memory_space=pltpu.VMEM),
        compiler_params=pltpu.CompilerParams(vmem_limit_bytes=4 * 2**20),
        cost_estimate=pl.CostEstimate(
            flops=0, bytes_accessed=4 * times * block.size, transcendentals=0
        ),
    )(block)


def sum_and_repeat_kernel(parts_ref, out_ref, rest_ref):
    times, _, columns = out_ref.shape
    total = parts_ref[0]
    for i in range(1, times):
        total = total + parts_ref[i]
    rest_ref[...] = total[:, columns:]
    for i in range(times):
        out_ref[i] = total[:, :columns]


def sum_and_repeat(parts, columns):
    times, rows, width = parts.shape
    vmem = pl.BlockSpec(memory_space=pltpu.VMEM)
    return pl.pallas_call(
        sum_and_repeat_kernel,
        out_shape=(
            jax.ShapeDtypeStruct((times, rows, columns), parts.dtype),
            jax.ShapeDtypeStruct((rows, width - columns), parts.dtype),
        ),
        in_specs=[vmem],
        out_specs=(vmem, vmem),
        compiler_params=pltpu.CompilerParams(vmem_limit_bytes=6 * 2**20),
        cost_estimate=pl.CostEstimate(
            flops=parts.size, bytes_accessed=8 * parts.size, transcendentals=0
        ),
    )(parts)


def per_device(momentum, gradient, weight, right_factor):
    summed = momentum + gradient.astype(jnp.float32)
    right_all = gather_over_row(repeat(right_factor, ROWS))
    projected = sum_over_col(product(summed, right_all, ((1,), (1,))))
    local_cross = product(projected, summed, ((0,), (0,)))
    half = RANK // 2
    local_gram = product(projected, projected, ((0,), (0,)))
    rows, columns = RANK // ROWS, summed.shape[1]
    at = band_index() * rows
    band = jnp.concatenate(
        [
            lax.dynamic_slice_in_dim(local_gram, at, rows, 0),
            lax.dynamic_slice_in_dim(local_gram, at + half, rows, 0)[:, half:],
        ],
        1,
    )
    bands = jnp.broadcast_to(band[None], (ROWS,) + band.shape)
    parts = jnp.concatenate([local_cross.reshape(ROWS, rows, -1), bands], axis=2)
    taken = lax.all_to_all(parts, "row", 0, 0)
    cross_copies, gram_band = sum_and_repeat(taken, columns)
    packed, cross_copies = gather_bands(gram_band, cross_copies)
    cross = gather_over_row(cross_copies)
    lower_inverse = inverse_factor(packed)
    right_product, squares = right_product_and_squares(lower_inverse, cross)
    squares = sum_small_over_col(squares)[0]
    ortho = product(projected, lower_inverse, ((1,), (1,)))
    momentum_delta = product(ortho, right_product, ((1,), (0,)), lax.Precision.HIGH)
    new_momentum = summed - (1.0 - momentum_keep) * momentum_delta
    inverse = lax.rsqrt(squares / NDIM + epsilon)
    factor_all = right_product * inverse[:, None]
    new_factor = lax.dynamic_slice_in_dim(
        factor_all, lax.axis_index("row") * right_factor.shape[0], right_factor.shape[0], 0
    )
    factor_all, new_factor = lax.optimization_barrier((factor_all, new_factor))
    weight_delta = product(ortho, factor_all, ((1,), (0,)), lax.Precision.HIGH)
    step_scale = learn_rate * math.sqrt(MDIM / RANK)
    new_weight = (1.0 - learn_rate * weight_decay) * weight - step_scale * weight_delta
    return (new_momentum, new_weight, new_factor)


def solution(mesh):
    in_specs = (P("row", "col"), P("row", "col"), P("row", "col"), P("row", "col"))
    out_specs = (P("row", "col"), P("row", "col"), P("row", "col"))
    return jax.shard_map(
        per_device, mesh=mesh, in_specs=in_specs, out_specs=out_specs, check_vma=False
    )
```

```python
import math

import jax
import jax.numpy as jnp
from jax import lax
from jax.experimental import pallas as pl
from jax.experimental.pallas import tpu as pltpu
from jax.sharding import PartitionSpec as P

MDIM = 7168
NDIM = 18432
RANK = 256

epsilon = 1e-06
momentum_keep = 0.95
learn_rate = 0.3
weight_decay = 0.1

HIGHEST = lax.Precision.HIGHEST

ROWS = 16
DEPTH = 8
Z_GROUPS = [[2 * z + core for z in range(DEPTH)] for core in range(2)]
CORE_SWAP = [(i, i ^ 1) for i in range(2 * DEPTH)]


def pairs_on(partner, others, index):
    return [(index(i, j), index(partner[i], j)) for i in range(len(partner)) for j in range(others)]


def z_pairs(partner):
    return pairs_on(partner, 2, lambda z, core: 2 * z + core)


Z_BUTTERFLY = (
    z_pairs([1, 0, 3, 2, 5, 4, 7, 6]),
    z_pairs([7, 2, 1, 4, 3, 6, 5, 0]),
    z_pairs([3, 6, 5, 0, 7, 2, 1, 4]),
)

def product(a, b, contract, precision=HIGHEST):
    return lax.dot_general(
        a, b, (contract, ((), ())), precision=precision, preferred_element_type=jnp.float32
    )


def gather_over_row(copies):
    block = copies[0]
    return lax.all_to_all(copies, "row", 0, 0).reshape((ROWS * block.shape[0],) + block.shape[1:])


def sum_over_row(whole):
    parts = whole.reshape((ROWS, whole.shape[0] // ROWS) + whole.shape[1:])
    return jnp.sum(lax.all_to_all(parts, "row", 0, 0), axis=0)


def sum_over_col(whole):
    core = lax.axis_index("col") % 2
    rows, columns = whole.shape
    half = columns // 2
    kept = lax.dynamic_slice_in_dim(whole, core * half, half, 1)
    given = lax.dynamic_slice_in_dim(whole, (1 - core) * half, half, 1)
    chip = kept + lax.ppermute(given, "col", CORE_SWAP)
    parts = chip.reshape(DEPTH, rows // DEPTH, half)
    part = jnp.sum(lax.all_to_all(parts, "col", 0, 0, axis_index_groups=Z_GROUPS), axis=0)
    copies = jnp.broadcast_to(part[None], (DEPTH,) + part.shape)
    mine = lax.all_to_all(copies, "col", 0, 0, axis_index_groups=Z_GROUPS).reshape(chip.shape)
    return in_order(core == 0, mine, lax.ppermute(mine, "col", CORE_SWAP), 1)


def in_order(first, mine, other, axis=0):
    return jnp.where(
        first, jnp.concatenate([mine, other], axis), jnp.concatenate([other, mine], axis)
    )


def band_index():
    place = lax.axis_index("col")
    return place % 2 * 4 + place // 2 % 4


def gather_bands(band, other):
    place = lax.axis_index("col")
    core, z = place % 2, place // 2
    band, other = lax.optimization_barrier((band, other))
    received = lax.ppermute(band, "col", Z_BUTTERFLY[0])
    mine = in_order(z % 2 == 0, band, received)
    mine = in_order(z // 2 % 2 == 0, mine, lax.ppermute(mine, "col", Z_BUTTERFLY[1]))
    return in_order(core == 0, mine, lax.ppermute(mine, "col", CORE_SWAP)), other


def sum_small_over_col(value):
    value = value + lax.ppermute(value, "col", CORE_SWAP)
    copies = jnp.broadcast_to(value[None], (DEPTH,) + value.shape)
    return jnp.sum(lax.all_to_all(copies, "col", 0, 0, axis_index_groups=Z_GROUPS), axis=0)


BAND = 32
SUB = 8
LANES = 128


def inverse_factor_kernel(gram_ref, out_ref, work):
    n = out_ref.shape[0]
    groups, tiles = BAND // SUB, n // LANES
    row_of = lax.broadcasted_iota(jnp.int32, (SUB, LANES), 0)
    half = n // 2
    work[:half, :] = gram_ref[:, :n]
    work[half:, :half] = jnp.zeros((n - half, half), jnp.float32)
    work[half:, half:] = gram_ref[:, n:]
    for start in range(0, n, BAND):
        columns = [
            [
                jnp.broadcast_to(
                    work[start + SUB * g : start + SUB * (g + 1), start + j : start + j + 1],
                    (SUB, LANES),
                )
                if g >= j // SUB
                else None
                for g in range(groups)
            ]
            for j in range(BAND)
        ]
        place = lax.broadcasted_iota(jnp.int32, (BAND, n), 1) - start
        identity = (place == lax.broadcasted_iota(jnp.int32, (BAND, n), 0)).astype(jnp.float32)
        band = jnp.where((place >= 0) & (place < BAND), identity, work[start : start + BAND, :])
        rows = [
            [band[SUB * g : SUB * (g + 1), LANES * t : LANES * (t + 1)] for t in range(tiles)]
            for g in range(groups)
        ]
        for k in range(BAND):
            own, at = divmod(k, SUB)
            pivot = jnp.broadcast_to(columns[k][own][at : at + 1, :], (SUB, LANES))
            root = lax.rsqrt(pivot)
            reciprocal = root * root
            for j in range(k + 1, BAND):
                g0, at_j = divmod(j, SUB)
                scale = jnp.broadcast_to(columns[k][g0][at_j : at_j + 1, :], (SUB, LANES)) * reciprocal
                for g in range(g0, groups):
                    columns[j][g] = columns[j][g] - columns[k][g] * scale
            row = [jnp.broadcast_to(rows[own][t][at : at + 1, :], (SUB, LANES)) for t in range(tiles)]
            scaled = [value * reciprocal for value in row]
            for g in range(own, groups):
                column = columns[k][g]
                if g == own:
                    column = jnp.where(row_of > at, column, 0.0)
                for t in range(tiles):
                    updated = rows[g][t] - column * scaled[t]
                    if g == own:
                        updated = jnp.where(row_of == at, row[t] * root, updated)
                    rows[g][t] = updated
        for g in range(groups):
            for t in range(tiles):
                work[start + SUB * g : start + SUB * (g + 1), LANES * t : LANES * (t + 1)] = rows[g][t]
        below = n - start - BAND
        if below:
            value = work[start : start + BAND, :]
            first = value.astype(jnp.bfloat16)
            rest = value - first.astype(jnp.float32)
            second = rest.astype(jnp.bfloat16)
            third = (rest - second.astype(jnp.float32)).astype(jnp.bfloat16)
            left = jnp.concatenate([first, first, second, second, first, third], 0)
            right = jnp.concatenate([first, second, first, second, third, first], 0)
            update = lax.dot_general(
                left[:, start + BAND :],
                right,
                (((0,), (0,)), ((), ())),
                preferred_element_type=jnp.float32,
            )
            place = lax.broadcasted_iota(jnp.int32, (below, n), 1) - start
            old = jnp.where((place >= 0) & (place < BAND), 0.0, work[start + BAND :, :])
            work[start + BAND :, :] = old - update
    row = lax.broadcasted_iota(jnp.int32, (n, n), 0)
    column = lax.broadcasted_iota(jnp.int32, (n, n), 1)
    out_ref[...] = jnp.where(row >= column, work[...], 0.0)


def inverse_factor(packed):
    n = 2 * packed.shape[0]
    return pl.pallas_call(
        inverse_factor_kernel,
        out_shape=jax.ShapeDtypeStruct((n, n), jnp.float32),
        in_specs=[pl.BlockSpec(memory_space=pltpu.VMEM)],
        out_specs=pl.BlockSpec(memory_space=pltpu.VMEM),
        scratch_shapes=[pltpu.VMEM((n, n), jnp.float32)],
        compiler_params=pltpu.CompilerParams(vmem_limit_bytes=6 * 2**20),
        cost_estimate=pl.CostEstimate(flops=2 * n**3, bytes_accessed=8 * n * n, transcendentals=n),
    )(packed)


def right_product_kernel(inverse_ref, cross_ref, out_ref, squares_ref):
    inverse = inverse_ref[...]
    total = jnp.zeros((inverse.shape[0], LANES), jnp.float32)
    for start in range(0, cross_ref.shape[1], 3 * LANES):
        value = product(inverse, cross_ref[:, start : start + 3 * LANES], ((1,), (0,)))
        out_ref[:, start : start + 3 * LANES] = value
        for at in range(0, 3 * LANES, LANES):
            total += value[:, at : at + LANES] * value[:, at : at + LANES]
    squares_ref[...] = jnp.sum(total.T, axis=0, keepdims=True)


def right_product_and_squares(inverse, cross):
    rank, columns = cross.shape
    vmem = pl.BlockSpec(memory_space=pltpu.VMEM)
    return pl.pallas_call(
        right_product_kernel,
        out_shape=(
            jax.ShapeDtypeStruct(cross.shape, jnp.float32),
            jax.ShapeDtypeStruct((1, rank), jnp.float32),
        ),
        in_specs=[vmem, vmem],
        out_specs=(vmem, vmem),
        compiler_params=pltpu.CompilerParams(vmem_limit_bytes=8 * 2**20),
        cost_estimate=pl.CostEstimate(
            flops=12 * rank * rank * columns, bytes_accessed=8 * cross.size, transcendentals=0
        ),
    )(inverse, cross)


def repeat_kernel(block_ref, out_ref):
    value = block_ref[...]
    for i in range(out_ref.shape[0]):
        out_ref[i] = value


def repeat(block, times):
    return pl.pallas_call(
        repeat_kernel,
        out_shape=jax.ShapeDtypeStruct((times,) + block.shape, block.dtype),
        in_specs=[pl.BlockSpec(memory_space=pltpu.VMEM)],
        out_specs=pl.BlockSpec(memory_space=pltpu.VMEM),
        compiler_params=pltpu.CompilerParams(vmem_limit_bytes=4 * 2**20),
        cost_estimate=pl.CostEstimate(
            flops=0, bytes_accessed=4 * times * block.size, transcendentals=0
        ),
    )(block)


def sum_and_repeat_kernel(parts_ref, out_ref, rest_ref):
    times, _, columns = out_ref.shape
    total = parts_ref[0]
    for i in range(1, times):
        total = total + parts_ref[i]
    rest_ref[...] = total[:, columns:]
    for i in range(times):
        out_ref[i] = total[:, :columns]


def sum_and_repeat(parts, columns):
    times, rows, width = parts.shape
    vmem = pl.BlockSpec(memory_space=pltpu.VMEM)
    return pl.pallas_call(
        sum_and_repeat_kernel,
        out_shape=(
            jax.ShapeDtypeStruct((times, rows, columns), parts.dtype),
            jax.ShapeDtypeStruct((rows, width - columns), parts.dtype),
        ),
        in_specs=[vmem],
        out_specs=(vmem, vmem),
        compiler_params=pltpu.CompilerParams(vmem_limit_bytes=6 * 2**20),
        cost_estimate=pl.CostEstimate(
            flops=parts.size, bytes_accessed=8 * parts.size, transcendentals=0
        ),
    )(parts)


def per_device(momentum, gradient, weight, right_factor):
    summed = momentum + gradient.astype(jnp.float32)
    right_all = gather_over_row(repeat(right_factor, ROWS))
    projected = sum_over_col(product(summed, right_all, ((1,), (1,))))
    local_cross = product(projected, summed, ((0,), (0,)))
    half = RANK // 2
    local_gram = product(projected, projected, ((0,), (0,)))
    rows, columns = RANK // ROWS, summed.shape[1]
    at = band_index() * rows
    band = jnp.concatenate(
        [
            lax.dynamic_slice_in_dim(local_gram, at, rows, 0),
            lax.dynamic_slice_in_dim(local_gram, at + half, rows, 0)[:, half:],
        ],
        1,
    )
    bands = jnp.broadcast_to(band[None], (ROWS,) + band.shape)
    parts = jnp.concatenate([local_cross.reshape(ROWS, rows, -1), bands], axis=2)
    taken = lax.all_to_all(parts, "row", 0, 0)
    cross_copies, gram_band = sum_and_repeat(taken, columns)
    packed, cross_copies = gather_bands(gram_band, cross_copies)
    cross = gather_over_row(cross_copies)
    lower_inverse = inverse_factor(packed)
    right_product, squares = right_product_and_squares(lower_inverse, cross)
    squares = sum_small_over_col(squares)[0]
    ortho = product(projected, lower_inverse, ((1,), (1,)))
    momentum_delta = product(ortho, right_product, ((1,), (0,)), lax.Precision.HIGH)
    new_momentum = summed - (1.0 - momentum_keep) * momentum_delta
    inverse = lax.rsqrt(squares / NDIM + epsilon)
    factor_all = right_product * inverse[:, None]
    new_factor = lax.dynamic_slice_in_dim(
        factor_all, lax.axis_index("row") * right_factor.shape[0], right_factor.shape[0], 0
    )
    factor_all, new_factor = lax.optimization_barrier((factor_all, new_factor))
    weight_delta = product(ortho, factor_all, ((1,), (0,)), lax.Precision.HIGH)
    step_scale = learn_rate * math.sqrt(MDIM / RANK)
    new_weight = (1.0 - learn_rate * weight_decay) * weight - step_scale * weight_delta
    return (new_momentum, new_weight, new_factor)


def solution(mesh):
    in_specs = (P("row", "col"), P("row", "col"), P("row", "col"), P("row", "col"))
    out_specs = (P("row", "col"), P("row", "col"), P("row", "col"))
    return jax.shard_map(
        per_device, mesh=mesh, in_specs=in_specs, out_specs=out_specs, check_vma=False
    )
```

```python
import math

import jax
import jax.numpy as jnp
from jax import lax
from jax.experimental import pallas as pl
from jax.experimental.pallas import tpu as pltpu
from jax.sharding import PartitionSpec as P

MDIM = 7168
NDIM = 18432
RANK = 256

epsilon = 1e-06
momentum_keep = 0.95
learn_rate = 0.3
weight_decay = 0.1

HIGHEST = lax.Precision.HIGHEST

ROWS = 16
DEPTH = 8
Z_GROUPS = [[2 * z + core for z in range(DEPTH)] for core in range(2)]
CORE_SWAP = [(i, i ^ 1) for i in range(2 * DEPTH)]


def pairs_on(partner, others, index):
    return [(index(i, j), index(partner[i], j)) for i in range(len(partner)) for j in range(others)]


def z_pairs(partner):
    return pairs_on(partner, 2, lambda z, core: 2 * z + core)


Z_BUTTERFLY = (
    z_pairs([1, 0, 3, 2, 5, 4, 7, 6]),
    z_pairs([7, 2, 1, 4, 3, 6, 5, 0]),
    z_pairs([3, 6, 5, 0, 7, 2, 1, 4]),
)

def product(a, b, contract, precision=HIGHEST):
    return lax.dot_general(
        a, b, (contract, ((), ())), precision=precision, preferred_element_type=jnp.float32
    )


def gather_over_row(copies):
    block = copies[0]
    return lax.all_to_all(copies, "row", 0, 0).reshape((ROWS * block.shape[0],) + block.shape[1:])


def sum_over_row(whole):
    parts = whole.reshape((ROWS, whole.shape[0] // ROWS) + whole.shape[1:])
    return jnp.sum(lax.all_to_all(parts, "row", 0, 0), axis=0)


def sum_over_col(whole):
    core = lax.axis_index("col") % 2
    rows, columns = whole.shape
    half = columns // 2
    first, second = whole[:, :half], whole[:, half:]
    kept, given = jnp.where(core == 0, first, second), jnp.where(core == 0, second, first)
    chip = kept + lax.ppermute(given, "col", CORE_SWAP)
    parts = chip.reshape(DEPTH, rows // DEPTH, half)
    part = jnp.sum(lax.all_to_all(parts, "col", 0, 0, axis_index_groups=Z_GROUPS), axis=0)
    copies = jnp.broadcast_to(part[None], (DEPTH,) + part.shape)
    mine = lax.all_to_all(copies, "col", 0, 0, axis_index_groups=Z_GROUPS).reshape(chip.shape)
    return in_order(core == 0, mine, lax.ppermute(mine, "col", CORE_SWAP), 1)


def in_order(first, mine, other, axis=0):
    return jnp.where(
        first, jnp.concatenate([mine, other], axis), jnp.concatenate([other, mine], axis)
    )


def band_index():
    place = lax.axis_index("col")
    return place % 2 * 4 + place // 2 % 4


def gather_bands(band, other):
    place = lax.axis_index("col")
    core, z = place % 2, place // 2
    band, other = lax.optimization_barrier((band, other))
    received = lax.ppermute(band, "col", Z_BUTTERFLY[0])
    mine = in_order(z % 2 == 0, band, received)
    mine = in_order(z // 2 % 2 == 0, mine, lax.ppermute(mine, "col", Z_BUTTERFLY[1]))
    return in_order(core == 0, mine, lax.ppermute(mine, "col", CORE_SWAP)), other


def sum_small_over_col(value):
    value = value + lax.ppermute(value, "col", CORE_SWAP)
    copies = jnp.broadcast_to(value[None], (DEPTH,) + value.shape)
    return jnp.sum(lax.all_to_all(copies, "col", 0, 0, axis_index_groups=Z_GROUPS), axis=0)


BAND = 32
SUB = 8
LANES = 128


def inverse_factor_kernel(gram_ref, out_ref, work):
    n = out_ref.shape[0]
    groups, tiles = BAND // SUB, n // LANES
    row_of = lax.broadcasted_iota(jnp.int32, (SUB, LANES), 0)
    half = n // 2
    work[:half, :] = gram_ref[:, :n]
    work[half:, :half] = jnp.zeros((n - half, half), jnp.float32)
    work[half:, half:] = gram_ref[:, n:]
    for start in range(0, n, BAND):
        columns = [
            [
                jnp.broadcast_to(
                    work[start + SUB * g : start + SUB * (g + 1), start + j : start + j + 1],
                    (SUB, LANES),
                )
                if g >= j // SUB
                else None
                for g in range(groups)
            ]
            for j in range(BAND)
        ]
        place = lax.broadcasted_iota(jnp.int32, (BAND, n), 1) - start
        identity = (place == lax.broadcasted_iota(jnp.int32, (BAND, n), 0)).astype(jnp.float32)
        band = jnp.where((place >= 0) & (place < BAND), identity, work[start : start + BAND, :])
        rows = [
            [band[SUB * g : SUB * (g + 1), LANES * t : LANES * (t + 1)] for t in range(tiles)]
            for g in range(groups)
        ]
        for k in range(BAND):
            own, at = divmod(k, SUB)
            pivot = jnp.broadcast_to(columns[k][own][at : at + 1, :], (SUB, LANES))
            root = lax.rsqrt(pivot)
            reciprocal = root * root
            for j in range(k + 1, BAND):
                g0, at_j = divmod(j, SUB)
                scale = jnp.broadcast_to(columns[k][g0][at_j : at_j + 1, :], (SUB, LANES)) * reciprocal
                for g in range(g0, groups):
                    columns[j][g] = columns[j][g] - columns[k][g] * scale
            row = [jnp.broadcast_to(rows[own][t][at : at + 1, :], (SUB, LANES)) for t in range(tiles)]
            scaled = [value * reciprocal for value in row]
            for g in range(own, groups):
                column = columns[k][g]
                if g == own:
                    column = jnp.where(row_of > at, column, 0.0)
                for t in range(tiles):
                    updated = rows[g][t] - column * scaled[t]
                    if g == own:
                        updated = jnp.where(row_of == at, row[t] * root, updated)
                    rows[g][t] = updated
        for g in range(groups):
            for t in range(tiles):
                work[start + SUB * g : start + SUB * (g + 1), LANES * t : LANES * (t + 1)] = rows[g][t]
        below = n - start - BAND
        if below:
            value = work[start : start + BAND, :]
            first = value.astype(jnp.bfloat16)
            rest = value - first.astype(jnp.float32)
            second = rest.astype(jnp.bfloat16)
            third = (rest - second.astype(jnp.float32)).astype(jnp.bfloat16)
            left = jnp.concatenate([first, first, second, second, first, third], 0)
            right = jnp.concatenate([first, second, first, second, third, first], 0)
            update = lax.dot_general(
                left[:, start + BAND :],
                right,
                (((0,), (0,)), ((), ())),
                preferred_element_type=jnp.float32,
            )
            place = lax.broadcasted_iota(jnp.int32, (below, n), 1) - start
            old = jnp.where((place >= 0) & (place < BAND), 0.0, work[start + BAND :, :])
            work[start + BAND :, :] = old - update
    row = lax.broadcasted_iota(jnp.int32, (n, n), 0)
    column = lax.broadcasted_iota(jnp.int32, (n, n), 1)
    out_ref[...] = jnp.where(row >= column, work[...], 0.0)


def inverse_factor(packed):
    n = 2 * packed.shape[0]
    return pl.pallas_call(
        inverse_factor_kernel,
        out_shape=jax.ShapeDtypeStruct((n, n), jnp.float32),
        in_specs=[pl.BlockSpec(memory_space=pltpu.VMEM)],
        out_specs=pl.BlockSpec(memory_space=pltpu.VMEM),
        scratch_shapes=[pltpu.VMEM((n, n), jnp.float32)],
        compiler_params=pltpu.CompilerParams(vmem_limit_bytes=6 * 2**20),
        cost_estimate=pl.CostEstimate(flops=2 * n**3, bytes_accessed=8 * n * n, transcendentals=n),
    )(packed)


def right_product_kernel(inverse_ref, cross_ref, out_ref, squares_ref):
    inverse = inverse_ref[...]
    total = jnp.zeros((inverse.shape[0], LANES), jnp.float32)
    for start in range(0, cross_ref.shape[1], 3 * LANES):
        value = product(inverse, cross_ref[:, start : start + 3 * LANES], ((1,), (0,)))
        out_ref[:, start : start + 3 * LANES] = value
        for at in range(0, 3 * LANES, LANES):
            total += value[:, at : at + LANES] * value[:, at : at + LANES]
    squares_ref[...] = jnp.sum(total.T, axis=0, keepdims=True)


def right_product_and_squares(inverse, cross):
    rank, columns = cross.shape
    vmem = pl.BlockSpec(memory_space=pltpu.VMEM)
    return pl.pallas_call(
        right_product_kernel,
        out_shape=(
            jax.ShapeDtypeStruct(cross.shape, jnp.float32),
            jax.ShapeDtypeStruct((1, rank), jnp.float32),
        ),
        in_specs=[vmem, vmem],
        out_specs=(vmem, vmem),
        compiler_params=pltpu.CompilerParams(vmem_limit_bytes=8 * 2**20),
        cost_estimate=pl.CostEstimate(
            flops=12 * rank * rank * columns, bytes_accessed=8 * cross.size, transcendentals=0
        ),
    )(inverse, cross)


def repeat_kernel(block_ref, out_ref):
    value = block_ref[...]
    for i in range(out_ref.shape[0]):
        out_ref[i] = value


def repeat(block, times):
    return pl.pallas_call(
        repeat_kernel,
        out_shape=jax.ShapeDtypeStruct((times,) + block.shape, block.dtype),
        in_specs=[pl.BlockSpec(memory_space=pltpu.VMEM)],
        out_specs=pl.BlockSpec(memory_space=pltpu.VMEM),
        compiler_params=pltpu.CompilerParams(vmem_limit_bytes=4 * 2**20),
        cost_estimate=pl.CostEstimate(
            flops=0, bytes_accessed=4 * times * block.size, transcendentals=0
        ),
    )(block)


def sum_and_repeat_kernel(parts_ref, out_ref, rest_ref):
    times, _, columns = out_ref.shape
    total = parts_ref[0]
    for i in range(1, times):
        total = total + parts_ref[i]
    rest_ref[...] = total[:, columns:]
    for i in range(times):
        out_ref[i] = total[:, :columns]


def sum_and_repeat(parts, columns):
    times, rows, width = parts.shape
    vmem = pl.BlockSpec(memory_space=pltpu.VMEM)
    return pl.pallas_call(
        sum_and_repeat_kernel,
        out_shape=(
            jax.ShapeDtypeStruct((times, rows, columns), parts.dtype),
            jax.ShapeDtypeStruct((rows, width - columns), parts.dtype),
        ),
        in_specs=[vmem],
        out_specs=(vmem, vmem),
        compiler_params=pltpu.CompilerParams(vmem_limit_bytes=6 * 2**20),
        cost_estimate=pl.CostEstimate(
            flops=parts.size, bytes_accessed=8 * parts.size, transcendentals=0
        ),
    )(parts)


def per_device(momentum, gradient, weight, right_factor):
    summed = momentum + gradient.astype(jnp.float32)
    right_all = gather_over_row(repeat(right_factor, ROWS))
    projected = sum_over_col(product(summed, right_all, ((1,), (1,))))
    local_cross = product(projected, summed, ((0,), (0,)))
    half = RANK // 2
    local_gram = product(projected, projected, ((0,), (0,)))
    rows, columns = RANK // ROWS, summed.shape[1]
    at = band_index() * rows
    band = jnp.concatenate(
        [
            lax.dynamic_slice_in_dim(local_gram, at, rows, 0),
            lax.dynamic_slice_in_dim(local_gram, at + half, rows, 0)[:, half:],
        ],
        1,
    )
    bands = jnp.broadcast_to(band[None], (ROWS,) + band.shape)
    parts = jnp.concatenate([local_cross.reshape(ROWS, rows, -1), bands], axis=2)
    taken = lax.all_to_all(parts, "row", 0, 0)
    cross_copies, gram_band = sum_and_repeat(taken, columns)
    packed, cross_copies = gather_bands(gram_band, cross_copies)
    cross = gather_over_row(cross_copies)
    lower_inverse = inverse_factor(packed)
    right_product, squares = right_product_and_squares(lower_inverse, cross)
    squares = sum_small_over_col(squares)[0]
    ortho = product(projected, lower_inverse, ((1,), (1,)))
    momentum_delta = product(ortho, right_product, ((1,), (0,)), lax.Precision.HIGH)
    new_momentum = summed - (1.0 - momentum_keep) * momentum_delta
    inverse = lax.rsqrt(squares / NDIM + epsilon)
    factor_all = right_product * inverse[:, None]
    new_factor = lax.dynamic_slice_in_dim(
        factor_all, lax.axis_index("row") * right_factor.shape[0], right_factor.shape[0], 0
    )
    factor_all, new_factor = lax.optimization_barrier((factor_all, new_factor))
    weight_delta = product(ortho, factor_all, ((1,), (0,)), lax.Precision.HIGH)
    step_scale = learn_rate * math.sqrt(MDIM / RANK)
    new_weight = (1.0 - learn_rate * weight_decay) * weight - step_scale * weight_delta
    return (new_momentum, new_weight, new_factor)


def solution(mesh):
    in_specs = (P("row", "col"), P("row", "col"), P("row", "col"), P("row", "col"))
    out_specs = (P("row", "col"), P("row", "col"), P("row", "col"))
    return jax.shard_map(
        per_device, mesh=mesh, in_specs=in_specs, out_specs=out_specs, check_vma=False
    )
```
